32 devices in a mesh: dp: 16 (over z, y, x), fsdp: 2 (over core).
Axes of the slice: x: 2, y: 2, z: 4, core: 2. Of those that a mesh axis runs over, the one named last changes fastest.
Arguments:
- activations: bfloat16 [8192, 8192], P('dp', 'fsdp'), may hold values from -6 to 6
- out_grads: bfloat16 [16, 896, 8192], P(None, 'fsdp', 'dp'), may hold values from -0.09375 to 0.09375
- proj_basis: bfloat16 [8192, 512], P('fsdp', 'dp'), may hold values from -0.0625 to 0.0625
- weight: bfloat16 [8192, 14336], P('fsdp', 'dp'), may hold values from -6 to 6
- ema_weight: bfloat16 [8192, 14336], P('fsdp', 'dp'), may hold values from -6 to 6
- first_moment: float32 [14336, 512], P(('dp', 'fsdp')), may hold values from -2 to 2
- second_moment: float32 [14336, 512], P(('dp', 'fsdp')), may hold values from 0.01 to 0.1
Outputs:
- new_weight: bfloat16 [8192, 14336], P('fsdp', 'dp')
- new_ema: bfloat16 [8192, 14336], P('fsdp', 'dp')
- new_first: float32 [14336, 512], P(('dp', 'fsdp'))
- new_second: float32 [14336, 512], P(('dp', 'fsdp'))
The draws below stay inside these ranges and needn't reach their ends.
All inputs are finite; a program needn't handle non-finite values.
Results may differ from the reference program's by a relative error of at most 0.0031.
Values may be sent and summed in bfloat16 or wider, within the bound.
A program may use at most 128 MiB of HBM per device.

```python
import math
import jax
import jax.numpy as jnp

D = 8192
FF = 14336
RANK = 512
TOKENS = 8192
N_DP = 16


def strengthened(drawn, own_key, source, target, parts, factor):
    owner, partner = [(jnp.arange(drawn.shape[axis_at]) // (drawn.shape[axis_at] // parts)).reshape([-1 if axis == axis_at else 1 for axis in range(drawn.ndim)]) for axis_at in (source, target)]
    chosen = jax.random.permutation(own_key, parts)[partner]
    strong = (owner == chosen) | (owner == (partner + parts // 2) % parts)
    return jnp.where(strong, factor * drawn, drawn)


def levels(key, dims, cuts, low, largest):
    factor_of, own = 1.0, jax.random.fold_in(key, 6)
    for dim, blocks in cuts:
        heights = jnp.exp(jax.random.uniform(jax.random.fold_in(own, dim), (blocks,), jnp.float32, low / len(cuts), largest / len(cuts)))
        factor_of = factor_of * jnp.repeat(heights, dims[dim] // blocks).reshape([-1 if axis == dim else 1 for axis in range(len(dims))])
    return factor_of


def centred(key, dims, scale, most, shards=(), held_as=jnp.bfloat16):
    result = scale * jax.random.normal(key, dims, jnp.float32)
    if shards:
        result = result * levels(key, dims, shards, -0.22, 0.18)
    return jnp.clip(result, -most, most).astype(held_as)


def bell_draw_with(rng, extent, width, bound, shards, heavy, kind=jnp.bfloat16):
    result = width * jax.random.normal(rng, extent, jnp.float32)
    if shards:
        result = result * levels(rng, extent, shards, -0.22, 0.18)
    return jnp.clip(strengthened(result, jax.random.fold_in(rng, 3), *heavy), -bound, bound).astype(kind)


def setup_inputs(seed: int = 0) -> dict:
    seeds = jax.random.split(jax.random.key(seed), 8)
    activations = centred(seeds[0], (TOKENS, D), 1.0, 6.0, ((0, 16), (1, 2)))
    out_grads = bell_draw_with(seeds[1], (N_DP, FF // N_DP, TOKENS), TOKENS ** -0.5, 0.09375, ((1, 2), (2, 16)), (2, 0, 16, 2.0))
    proj_basis = centred(seeds[2], (D, RANK), D ** -0.5, 0.0625, ((0, 2), (1, 16)))
    weight = centred(seeds[3], (D, FF), 1.0, 6.0, ((0, 2), (1, 16)))
    ema_weight = centred(seeds[4], (D, FF), 1.0, 6.0, ((0, 2), (1, 16)))
    first_moment = centred(seeds[5], (FF, RANK), 0.3, 2.0, ((0, 32),), jnp.float32)
    second_moment = jnp.clip(jnp.exp(math.log(0.1) - 2.3025851 * jax.random.uniform(seeds[6], (FF, RANK), jnp.float32) ** levels(seeds[6], (FF, RANK), ((0, 32),), -0.2, 0.2)), 0.01, 0.1)
    return dict(activations=activations, out_grads=out_grads, proj_basis=proj_basis, weight=weight, ema_weight=ema_weight, first_moment=first_moment, second_moment=second_moment)


def reference(activations, out_grads, proj_basis, weight, ema_weight, first_moment, second_moment):
    projected = jnp.dot(activations, proj_basis, preferred_element_type=jnp.float32).astype(jnp.bfloat16)
    grad_rows = out_grads.reshape(FF, TOKENS)
    proj_grads = jnp.dot(grad_rows, projected, preferred_element_type=jnp.float32)
    new_first = 0.9 * first_moment + 0.1 * proj_grads
    new_second = 0.95 * second_moment + 0.05 * proj_grads * proj_grads
    direction = (new_first / jnp.sqrt(new_second)).astype(jnp.bfloat16)
    update = jnp.dot(proj_basis, direction.T, preferred_element_type=jnp.float32)
    stepped = weight.astype(jnp.float32) - 0.2 * update
    new_ema = (0.9 * ema_weight.astype(jnp.float32) + 0.1 * stepped).astype(jnp.bfloat16)
    return (stepped.astype(jnp.bfloat16), new_ema, new_first, new_second)
```

```python
import jax
import jax.numpy as jnp
from jax import lax
from jax.sharding import PartitionSpec as P

SHARES = (4, 4, 3, 3)


def pieces(whole, unit):
    if whole % unit:
        return [(0, whole)]
    count, total, ends = whole // unit, sum(SHARES), [0]
    for at in range(len(SHARES)):
        ends.append(count * sum(SHARES[: at + 1]) // total)
    return [(low * unit, high * unit) for low, high in zip(ends, ends[1:]) if high > low]


def order_of(at, bits):
    low = list(range(min(2, bits)))
    rest = list(range(len(low), bits))
    return (low if at % 2 == 0 else low[::-1]) + rest


def swap(value, bit, size):
    return lax.ppermute(value, "dp", [(i, i ^ (1 << bit)) for i in range(size)])


def gathered(block, order, size):
    me = lax.axis_index("dp")
    done, held = [], block
    for bit in order[::-1]:
        other = swap(held, bit, size)
        axis = sum(b > bit for b in done)
        mine = (me >> bit) & 1
        held = jnp.where(mine == 0, jnp.stack([held, other], axis), jnp.stack([other, held], axis))
        done.append(bit)
    return held.reshape((-1,) + block.shape[1:])


def scattered(grads, projected, order, size):
    me = lax.axis_index("dp")
    bits = len(order)
    left = list(range(bits))[::-1]

    def term(part, kind):
        out = jnp.einsum("...kt,tr->...kr", part, projected, preferred_element_type=jnp.float32)
        return out.astype(kind)

    held = grads.reshape((2,) * bits + grads.shape[1:])
    for step, bit in enumerate(order):
        axis, mine = left.index(bit), (me >> bit) & 1
        keep = lax.dynamic_index_in_dim(held, mine, axis, keepdims=False)
        give = lax.dynamic_index_in_dim(held, 1 - mine, axis, keepdims=False)
        if step == 0:
            other = swap(term(give, jnp.bfloat16), bit, size)
            keep = term(keep, jnp.float32)
        else:
            other = swap(give.astype(jnp.bfloat16), bit, size)
        held = keep + other.astype(jnp.float32)
        left.remove(bit)
    return held


def make(size):
    bits = size.bit_length() - 1

    def on_device(activations, out_grads, proj_basis, weight, ema_weight, first_moment, second_moment):
        features = proj_basis.shape[0]
        turned = proj_basis.T
        partial_value, columns = 0.0, []
        for at, (low, high) in enumerate(pieces(features, 128)):
            part = gathered(turned[:, low:high], order_of(at, bits), size)
            columns.append(part)
            partial_value += lax.dot_general(
                activations[:, low:high], part, (((1,), (1,)), ((), ())), preferred_element_type=jnp.float32
            )
        full_basis = jnp.concatenate(columns, axis=1)
        projected = lax.psum(partial_value, "fsdp").astype(jnp.bfloat16)
        proj_grads = jnp.concatenate(
            [
                scattered(out_grads[:, low:high], projected, order_of(at, bits), size)
                for at, (low, high) in enumerate(pieces(out_grads.shape[1], 16))
            ],
            axis=0,
        )
        new_first = 0.9 * first_moment + 0.1 * proj_grads
        new_second = 0.95 * second_moment + 0.05 * proj_grads * proj_grads
        direction = (new_first / jnp.sqrt(new_second)).astype(jnp.bfloat16)
        update = lax.dot_general(
            full_basis,
            lax.all_gather(direction, "fsdp", axis=0, tiled=True),
            (((0,), (1,)), ((), ())),
            preferred_element_type=jnp.float32,
        )
        stepped = weight.astype(jnp.float32) - 0.2 * update
        new_ema = (0.9 * ema_weight.astype(jnp.float32) + 0.1 * stepped).astype(jnp.bfloat16)
        return (stepped.astype(jnp.bfloat16), new_ema, new_first, new_second)

    return on_device


def solution(mesh):
    in_specs = (
        P("dp", "fsdp"),
        P(None, "fsdp", "dp"),
        P("fsdp", "dp"),
        P("fsdp", "dp"),
        P("fsdp", "dp"),
        P(("dp", "fsdp"), None),
        P(("dp", "fsdp"), None),
    )
    out_specs = (P("fsdp", "dp"), P("fsdp", "dp"), P(("dp", "fsdp"), None), P(("dp", "fsdp"), None))
    return jax.shard_map(
        make(mesh.shape["dp"]), mesh=mesh, in_specs=in_specs, out_specs=out_specs, check_vma=False
    )
```

```python
import jax
import jax.numpy as jnp
from jax import lax
from jax.sharding import PartitionSpec as P

SHARES = (1, 1, 1)
ORDERS = ((0, 2, 1), (1, 0, 2), (2, 1, 0))


def pieces(whole, unit):
    if whole % unit or whole // unit < len(SHARES):
        return [(0, whole)]
    count, total, ends = whole // unit, sum(SHARES), [0]
    for at in range(len(SHARES)):
        ends.append(count * sum(SHARES[: at + 1]) // total)
    return [(low * unit, high * unit) for low, high in zip(ends, ends[1:]) if high > low]


def swap(value, bit, size):
    return lax.ppermute(value, "dp", [(i, i ^ (1 << bit)) for i in range(size)])


def bit_of(bit):
    return (lax.axis_index("dp") >> bit) & 1


def grown(held, bit, done, size):
    other, mine = swap(held, bit, size), bit_of(bit)
    axis = sum(b > bit for b in done)
    done.append(bit)
    return jnp.where(mine == 0, jnp.stack([held, other], axis), jnp.stack([other, held], axis))


def turns(bits):
    own = min(3, bits)
    return [[bit for bit in order if bit < own] for order in ORDERS], list(range(own, bits))


def gathered(block, bits, size, grads):
    orders, shared = turns(bits)
    cuts = pieces(block.shape[1], 128)
    held, first = block, []
    for bit in shared[::-1]:
        held = grown(held, bit, first, size)
    parts = []
    for at, (start, end) in enumerate(cuts):
        part, done = held[..., start:end], list(first)
        for turn, bit in enumerate(orders[at][::-1]):
            if at == 0 and turn == len(orders[at]) - 1:
                part, grads = lax.optimization_barrier((part, grads))
            part = grown(part, bit, done, size)
        parts.append(part.reshape(-1, end - start))
    return cuts, parts, grads


def shrunk(held, bit, left, size):
    axis, mine = left.index(bit), bit_of(bit)
    left.remove(bit)
    keep = lax.dynamic_index_in_dim(held, mine, axis, keepdims=False)
    give = lax.dynamic_index_in_dim(held, 1 - mine, axis, keepdims=False)
    return keep + swap(give.astype(jnp.bfloat16), bit, size).astype(jnp.float32)


def started(grads, projected, bit, left, size):
    axis, mine = left.index(bit), bit_of(bit)
    left.remove(bit)

    def term(which, kind):
        part = lax.dynamic_index_in_dim(grads, which, axis, keepdims=False)
        out = jnp.einsum("...kt,tr->...kr", part, projected, preferred_element_type=jnp.float32)
        return out.astype(kind)

    other = swap(term(1 - mine, jnp.bfloat16), bit, size)
    return term(mine, jnp.float32) + other.astype(jnp.float32)


def scattered(grads, projected, bits, size):
    orders, shared = turns(bits)
    sums = []
    for at, (start, end) in enumerate(pieces(grads.shape[1], 16)):
        part = grads[:, start:end].reshape((2,) * bits + (end - start, grads.shape[2]))
        left = list(range(bits))[::-1]
        held = started(part, projected, orders[at][0], left, size)
        for bit in orders[at][1:]:
            held = shrunk(held, bit, left, size)
        sums.append(held)
    total = jnp.concatenate(sums, axis=-2)
    for bit in shared:
        total = shrunk(total, bit, left, size)
    return total


def summed(value, devices):
    if devices == 2:
        return value + lax.ppermute(value, "fsdp", [(0, 1), (1, 0)])
    return lax.psum(value, "fsdp")


def make(size, devices):
    bits = size.bit_length() - 1

    def on_device(activations, out_grads, proj_basis, weight, ema_weight, first_moment, second_moment):
        cuts, columns, out_grads = gathered(proj_basis.T, bits, size, out_grads)
        partial_value = 0.0
        for (low, high), part in zip(cuts, columns):
            partial_value += lax.dot_general(
                activations[:, low:high], part, (((1,), (1,)), ((), ())), preferred_element_type=jnp.float32
            )
        full_basis = jnp.concatenate(columns, axis=1)
        projected = summed(partial_value, devices).astype(jnp.bfloat16)
        proj_grads = scattered(out_grads, projected, bits, size)
        new_first = 0.9 * first_moment + 0.1 * proj_grads
        new_second = 0.95 * second_moment + 0.05 * proj_grads * proj_grads
        direction = (new_first / jnp.sqrt(new_second)).astype(jnp.bfloat16)
        update = lax.dot_general(
            full_basis,
            lax.all_gather(direction, "fsdp", axis=0, tiled=True),
            (((0,), (1,)), ((), ())),
            preferred_element_type=jnp.float32,
        )
        stepped = weight.astype(jnp.float32) - 0.2 * update
        new_ema = (0.9 * ema_weight.astype(jnp.float32) + 0.1 * stepped).astype(jnp.bfloat16)
        return (stepped.astype(jnp.bfloat16), new_ema, new_first, new_second)

    return on_device


def solution(mesh):
    in_specs = (
        P("dp", "fsdp"),
        P(None, "fsdp", "dp"),
        P("fsdp", "dp"),
        P("fsdp", "dp"),
        P("fsdp", "dp"),
        P(("dp", "fsdp"), None),
        P(("dp", "fsdp"), None),
    )
    out_specs = (P("fsdp", "dp"), P("fsdp", "dp"), P(("dp", "fsdp"), None), P(("dp", "fsdp"), None))
    return jax.shard_map(
        make(mesh.shape["dp"], mesh.shape["fsdp"]), mesh=mesh, in_specs=in_specs, out_specs=out_specs, check_vma=False
    )
```

```python
import jax
import jax.numpy as jnp
from jax import lax
from jax.sharding import PartitionSpec as P

SHARES = (1, 1, 1)
ORDERS = ((0, 2, 1), (1, 0, 2), (2, 1, 0))


def pieces(whole, unit):
    if whole % unit or whole // unit < len(SHARES):
        return [(0, whole)]
    count, total, ends = whole // unit, sum(SHARES), [0]
    for at in range(len(SHARES)):
        ends.append(-(-count * sum(SHARES[: at + 1]) // total))
    return [(low * unit, high * unit) for low, high in zip(ends, ends[1:]) if high > low]


def swap(value, bit, size):
    return lax.ppermute(value, "dp", [(i, i ^ (1 << bit)) for i in range(size)])


def bit_of(bit):
    return (lax.axis_index("dp") >> bit) & 1


def grown(held, bit, done, size):
    other, mine = swap(held, bit, size), bit_of(bit)
    axis = sum(b > bit for b in done)
    done.append(bit)
    return jnp.where(mine == 0, jnp.stack([held, other], axis), jnp.stack([other, held], axis))


def turns(bits):
    own = min(3, bits)
    return [[bit for bit in order if bit < own] for order in ORDERS], list(range(own, bits))


def gathered(block, bits, size, grads):
    orders, shared = turns(bits)
    cuts = pieces(block.shape[1], 128)
    held, first = block, []
    for bit in shared[::-1]:
        held = grown(held, bit, first, size)
    parts = []
    for at, (start, end) in enumerate(cuts):
        part, done = held[..., start:end], list(first)
        for turn, bit in enumerate(orders[at][::-1]):
            if at == 0 and turn == len(orders[at]) - 1:
                part, grads = lax.optimization_barrier((part, grads))
            part = grown(part, bit, done, size)
        parts.append(part.reshape(-1, end - start))
    slices = []
    for order, (start, end) in zip(orders, pieces(grads.shape[1], 16)):
        part = grads[:, start:end].reshape((2,) * bits + (end - start, grads.shape[2]))
        axis, mine = bits - 1 - order[0], bit_of(order[0])
        slices.append([lax.dynamic_index_in_dim(part, which, axis, keepdims=False) for which in (mine, 1 - mine)])
    parts[0], slices = lax.optimization_barrier((parts[0], slices))
    return cuts, parts, slices


def shrunk(held, bit, left, size):
    axis, mine = left.index(bit), bit_of(bit)
    left.remove(bit)
    keep = lax.dynamic_index_in_dim(held, mine, axis, keepdims=False)
    give = lax.dynamic_index_in_dim(held, 1 - mine, axis, keepdims=False)
    return keep + swap(give.astype(jnp.bfloat16), bit, size).astype(jnp.float32)


def started(halves, projected, bit, left, size):
    left.remove(bit)

    def term(part, kind):
        out = jnp.einsum("...kt,tr->...kr", part, projected, preferred_element_type=jnp.float32)
        return out.astype(kind)

    other = swap(term(halves[1], jnp.bfloat16), bit, size)
    return term(halves[0], jnp.float32) + other.astype(jnp.float32)


def scattered(grads, projected, bits, size):
    orders, shared = turns(bits)
    sums = []
    for at, part in enumerate(grads):
        left = list(range(bits))[::-1]
        held = started(part, projected, orders[at][0], left, size)
        for bit in orders[at][1:]:
            held = shrunk(held, bit, left, size)
        sums.append(held)
    total = jnp.concatenate(sums, axis=-2)
    for bit in shared:
        total = shrunk(total, bit, left, size)
    return total


def summed(value, devices):
    if devices == 2:
        return value + lax.ppermute(value, "fsdp", [(0, 1), (1, 0)])
    return lax.psum(value, "fsdp")


def make(size, devices):
    bits = size.bit_length() - 1

    def on_device(activations, out_grads, proj_basis, weight, ema_weight, first_moment, second_moment):
        cuts, columns, grads = gathered(proj_basis.T, bits, size, out_grads)
        partial_value = 0.0
        for (low, high), part in zip(cuts, columns):
            partial_value += lax.dot_general(
                activations[:, low:high], part, (((1,), (1,)), ((), ())), preferred_element_type=jnp.float32
            )
        full_basis = jnp.concatenate(columns, axis=1)
        projected = summed(partial_value, devices).astype(jnp.bfloat16)
        proj_grads = scattered(grads, projected, bits, size)
        new_first = 0.9 * first_moment + 0.1 * proj_grads
        new_second = 0.95 * second_moment + 0.05 * proj_grads * proj_grads
        direction = (new_first / jnp.sqrt(new_second)).astype(jnp.bfloat16)
        update = lax.dot_general(
            full_basis,
            lax.all_gather(direction, "fsdp", axis=0, tiled=True),
            (((0,), (1,)), ((), ())),
            preferred_element_type=jnp.float32,
        )
        stepped = weight.astype(jnp.float32) - 0.2 * update
        new_ema = (0.9 * ema_weight.astype(jnp.float32) + 0.1 * stepped).astype(jnp.bfloat16)
        return (stepped.astype(jnp.bfloat16), new_ema, new_first, new_second)

    return on_device


def solution(mesh):
    in_specs = (
        P("dp", "fsdp"),
        P(None, "fsdp", "dp"),
        P("fsdp", "dp"),
        P("fsdp", "dp"),
        P("fsdp", "dp"),
        P(("dp", "fsdp"), None),
        P(("dp", "fsdp"), None),
    )
    out_specs = (P("fsdp", "dp"), P("fsdp", "dp"), P(("dp", "fsdp"), None), P(("dp", "fsdp"), None))
    return jax.shard_map(
        make(mesh.shape["dp"], mesh.shape["fsdp"]), mesh=mesh, in_specs=in_specs, out_specs=out_specs, check_vma=False
    )
```
